32 devices in a mesh: seq: 8 (over z, x), head: 4 (over y, core).
Axes of the slice: x: 2, y: 2, z: 4, core: 2. Of those that a mesh axis runs over, the one named last changes fastest.
Arguments:
- query_rows: bfloat16 [4096, 4096], P(('seq', 'head')), may hold values from -6 to 6
- key_rows: bfloat16 [4096, 4096], P(('seq', 'head')), may hold values from -6 to 6
- value_rows: bfloat16 [4096, 4096], P(('seq', 'head')), may hold values from -6 to 6
- write_rate: bfloat16 [4096, 32], P(('seq', 'head')), may hold values from 0 to 1
- log_decay: bfloat16 [4096, 32], P(('seq', 'head')), may hold values from -1.5 to 0
Outputs:
- head_output: bfloat16 [4096, 4096], P(('seq', 'head'))
The draws below stay inside these ranges and needn't reach their ends.
All inputs are finite; a program needn't handle non-finite values.
Results may differ from the reference program's by a relative error of at most 0.00105.
Values may be sent and summed in bfloat16 or wider, within the bound.
A program may use at most 128 MiB of HBM per device.

```python
import jax
import jax.numpy as jnp
from jax import lax

H = 32
DK = 128
DV = 128
GROUP = 128
TOK_DEV = 128
TOKENS = 4096


def head_kinds(key):
    share = 0.5
    return jax.random.uniform(jax.random.fold_in(key, 11), (H,)) < share


def log_uniform(key, extent, lower, upper):
    return jnp.exp(jax.random.uniform(key, extent, jnp.float32, jnp.log(lower), jnp.log(upper)))


def draw_log_decay(key, part):
    fast_heads = head_kinds(key)
    streams = jax.random.split(jax.random.fold_in(key, 23), 6)
    fast_rate = 1.0 / jax.random.uniform(streams[0], (H,), jnp.float32, 30.0, 50.0)
    slow_total = log_uniform(streams[1], (H,), 0.05, 0.3)
    rough_approximation = jax.random.uniform(streams[2], (TOKENS, H), jnp.float32, 0.5, 1.5)
    update_speed_entries = jnp.where(fast_heads, fast_rate, slow_total / TOKENS)
    accelerator_segments = log_uniform(streams[3], (TOKENS // TOK_DEV, 1, H), 0.5, 2.0)
    accelerator_segments = jnp.broadcast_to(accelerator_segments, (TOKENS // TOK_DEV, TOK_DEV, H)).reshape(TOKENS, H)
    segment_assignment = jax.random.randint(streams[4], (2, H), 0, TOKENS)
    forgetting_factor = jax.random.uniform(streams[5], (2, H), jnp.float32, 0.6, 0.8)
    sequence_indices = jnp.arange(TOKENS, dtype=jnp.int32)[:, None, None]
    element_cluster_sets = jnp.sum(jnp.where(sequence_indices == segment_assignment[None], jnp.log(forgetting_factor)[None], 0.0), axis=1)
    return (-update_speed_entries[None, :] * rough_approximation * accelerator_segments + element_cluster_sets).astype(jnp.bfloat16)


def draw_write_rate(key, part):
    fast_heads = head_kinds(key)
    streams = jax.random.split(jax.random.fold_in(key, 37), 3)
    fast_level = jax.random.uniform(streams[0], (H,), jnp.float32, 0.3, 0.8)
    slow_level = DK / TOKENS * log_uniform(streams[1], (H,), 0.2, 1.0)
    rough_approximation = jax.random.uniform(streams[2], (TOKENS, H), jnp.float32, 0.5, 1.2)
    return (jnp.where(fast_heads, fast_level, slow_level)[None, :] * rough_approximation).astype(jnp.bfloat16)


def shard_levels(stream_key, shape, pieces, least, high):
    gain = 1.0
    for position, shards_of in pieces:
        steps = jax.random.uniform(jax.random.fold_in(jax.random.fold_in(stream_key, 6), position), (shards_of,), jnp.float32, least / len(pieces), high / len(pieces))
        gain = gain * jnp.repeat(jnp.exp(steps), shape[position] // shards_of).reshape((-1,) + (1,) * (len(shape) - 1 - position))
    return gain


def gaussian(own_key, shape, scale, bound, pieces=(), held_as=jnp.bfloat16):
    loudness = shard_levels(own_key, shape, pieces, -0.22, 0.18) if pieces else 1.0
    entries = jax.random.normal(own_key, shape, jnp.float32) * scale * loudness
    return jnp.minimum(jnp.maximum(entries, -bound), bound).astype(held_as)


def setup_inputs(seed: int = 0) -> dict:
    arg_keys = jax.random.split(jax.random.key(seed), 6)
    query_rows = gaussian(arg_keys[0], (TOKENS, H * DK), 1.0, 6.0, ((0, 32),))
    key_rows = gaussian(arg_keys[1], (TOKENS, H * DK), 1.0, 6.0, ((0, 32),))
    value_rows = gaussian(arg_keys[2], (TOKENS, H * DV), 1.0, 6.0, ((0, 32),))
    write_rate = draw_write_rate(jax.random.fold_in(arg_keys[5], 71), 0)
    log_decay = draw_log_decay(jax.random.fold_in(arg_keys[5], 71), 0)
    return {"query_rows": query_rows, "key_rows": key_rows, "value_rows": value_rows, "write_rate": write_rate, "log_decay": log_decay}


highest = lax.Precision.HIGHEST
epsilon = 1e-06

def unit_rows(matrix):
    return matrix * lax.rsqrt(lax.optimization_barrier(jnp.sum(matrix * matrix, axis=-1, keepdims=True)) + epsilon)

def block_pieces(unit_keys, write_level, cumulative, values_f):
    block_len = unit_keys.shape[1]
    row_ids = lax.broadcasted_iota(jnp.int32, (block_len, block_len), 0)
    col_ids = lax.broadcasted_iota(jnp.int32, (block_len, block_len), 1)
    within = row_ids >= col_ids
    spread = cumulative[:, :, None] - cumulative[:, None, :]
    ratios = jnp.where(within, jnp.exp(jnp.where(within, spread, 0.0)), 0.0)
    gram = jnp.einsum('bia,bja->bij', unit_keys, unit_keys, precision=highest)
    system = jnp.where(row_ids > col_ids, write_level[:, :, None] * ratios * gram, 0.0) + jnp.eye(block_len, dtype=gram.dtype)
    growth = jnp.exp(cumulative)
    right_side = jnp.concatenate([write_level[:, :, None] * values_f, (write_level * growth)[:, :, None] * unit_keys], axis=2)
    solved = jax.scipy.linalg.solve_triangular(system, right_side, lower=True, unit_diagonal=True)
    value_width = values_f.shape[2]
    carried = unit_keys * jnp.exp(cumulative[:, -1:] - cumulative)[:, :, None]
    return (solved[:, :, :value_width], solved[:, :, value_width:], carried, growth, ratios)

def reference(query_rows, key_rows, value_rows, write_rate, log_decay):
    token_count = query_rows.shape[0]
    query_heads = query_rows.reshape(token_count, H, DK)
    key_heads = key_rows.reshape(token_count, H, DK)
    value_heads = value_rows.reshape(token_count, H, DV)

    def one_head(head_index):
        query_f = lax.dynamic_index_in_dim(query_heads, head_index, 1, False).astype(jnp.float32).reshape(-1, GROUP, DK)
        key_f = lax.dynamic_index_in_dim(key_heads, head_index, 1, False).astype(jnp.float32)
        unit_keys = unit_rows(key_f).reshape(-1, GROUP, DK)
        values_f = lax.dynamic_index_in_dim(value_heads, head_index, 1, False).astype(jnp.float32).reshape(-1, GROUP, DV)
        write_level = lax.dynamic_index_in_dim(write_rate, head_index, 1, False).astype(jnp.float32).reshape(-1, GROUP)
        decay_f = lax.dynamic_index_in_dim(log_decay, head_index, 1, False).astype(jnp.float32).reshape(-1, GROUP)
        cumulative = jnp.cumsum(decay_f, axis=1)
        base_new, wy_rows, carried, growth, ratios = block_pieces(unit_keys, write_level, cumulative, values_f)
        scores = jnp.einsum('bia,bja->bij', query_f, unit_keys, precision=highest) * ratios
        query_grown = query_f * growth[:, :, None]
        end_growth = jnp.exp(cumulative[:, -1])

        def advance(carry_state, member):
            base_c, wy_c, carried_c, grown_c, scores_c, end_c = member
            fresh = base_c - jnp.dot(wy_c, carry_state, precision=highest)
            emitted = jnp.dot(grown_c, carry_state, precision=highest) + jnp.dot(scores_c, fresh, precision=highest)
            next_state = end_c * carry_state + jnp.dot(carried_c.T, fresh, precision=highest)
            return (next_state, emitted)
        zero_state = jnp.zeros((DK, DV), jnp.float32)
        final_state, emitted = lax.scan(advance, zero_state, (base_new, wy_rows, carried, query_grown, scores, end_growth))
        return emitted.reshape(-1, DV).astype(jnp.bfloat16)
    per_head = lax.map(one_head, jnp.arange(H, dtype=jnp.int32))
    return jnp.swapaxes(per_head, 0, 1).reshape(token_count, H * DV)
```

```python
import functools

import jax
import jax.numpy as jnp
from jax import lax
from jax.experimental import pallas as pl
from jax.experimental.pallas import tpu as pltpu
from jax.sharding import PartitionSpec as P

LANES = 128
EPSILON = 1e-06
MESH = pl.DeviceIdType.MESH
F32 = jnp.float32
BF16 = jnp.bfloat16


def halves(x):
    high = x.astype(BF16)
    return high, (x - high.astype(F32)).astype(BF16)


def dot(a, b):
    return jnp.dot(a, b, preferred_element_type=F32)


def dot_t(a, b, dims):
    return lax.dot_general(a, b, (dims, ((), ())), preferred_element_type=F32)


def left3(a):
    high, low = halves(a)
    return jnp.concatenate([high, low, high], axis=1)


def right3(b):
    high, low = halves(b)
    return jnp.concatenate([high, high, low], axis=0)


def dot3(a, b):
    return dot(left3(a), right3(b))


def block_maps(keys, queries, values, beta_col, beta_row, cum_col, cum_row, row, col):
    gram = dot_t(keys, keys, ((1,), (1,)))
    raw_scores = dot_t(queries, keys, ((1,), (1,)))
    diagonal = jnp.where(row == col, gram, 0.0)
    r_col = lax.rsqrt(jnp.sum(diagonal, axis=1, keepdims=True) + EPSILON)
    r_row = lax.rsqrt(jnp.sum(diagonal, axis=0, keepdims=True) + EPSILON)
    within = row >= col
    ratios = jnp.where(within, jnp.exp(jnp.where(within, cum_col - cum_row, 0.0)), 0.0)
    faded = ratios * r_row
    lower = jnp.where(row > col, gram * faded * (beta_col * r_col), 0.0)
    scores = raw_scores * faded
    apart = row ^ col
    inverse = jnp.where(row == col, 1.0, 0.0) - jnp.where(apart == 1, lower, 0.0)
    span = 2
    while span < LANES:
        corner = jnp.where((apart >= span) & (apart < 2 * span), lower, 0.0)
        partial = dot3(corner, inverse)
        inverse = inverse - dot3(inverse, partial)
        span *= 2
    growth_col = jnp.exp(cum_col)
    growth_row = jnp.exp(cum_row)
    end_log = cum_row[:, LANES - 1 :]
    for_values = jnp.concatenate(halves(inverse * beta_row), axis=1)
    for_keys = jnp.concatenate(halves(inverse * (beta_row * growth_row * r_row)), axis=1)
    base = dot(for_values, jnp.concatenate([values, values], axis=0))
    wy = dot(for_keys, jnp.concatenate([keys, keys], axis=0))
    solved = jnp.concatenate([wy, base], axis=1)
    read = dot3(scores, solved)
    carried = solved * (r_col * jnp.exp(end_log - cum_col))
    left = dot_t(
        jnp.concatenate([keys, keys], axis=0),
        jnp.concatenate(halves(carried), axis=0),
        ((0,), (0,)),
    )
    end = jnp.exp(end_log)
    move = jnp.where(row == col, end, 0.0) - left[:, :LANES]
    query = queries.astype(F32) * growth_col - read[:, :LANES]
    return query, read[:, LANES:], move, left[:, LANES:]


def kernel(
    ranks, members, heads,
    q_ref, k_ref, v_ref, gate_ref,
    out_ref,
    q_in, k_in, v_in, gate_in, cum, cum_t, beta_t, state_in, state_out, read_map, read_base, staged,
    gate_send, gate_recv, part_send, part_recv, own_sem,
    state_send, state_recv, out_send, out_recv, own_out,
):
    rank, member = lax.axis_index("seq"), lax.axis_index("head")
    following, leading = lax.rem(rank + 1, ranks), lax.rem(rank + ranks - 1, ranks)
    sources, parts = (q_ref, k_ref, v_ref), (q_in, k_in, v_in)

    barrier = pltpu.get_barrier_semaphore()
    for away in range(1, members):
        pl.semaphore_signal(
            barrier, inc=1, device_id=(rank, lax.rem(member + away, members)), device_id_type=MESH
        )
    for other in (following, leading):
        pl.semaphore_signal(barrier, inc=1, device_id=(other, member), device_id_type=MESH)
    pl.semaphore_wait(barrier, members + 1)

    def columns(owner, i):
        return pl.ds(pl.multiple_of((owner * heads + i) * LANES, LANES), LANES)

    def gate_copy(away):
        target = lax.rem(member + away, members)
        return pltpu.make_async_remote_copy(
            src_ref=gate_ref.at[target], dst_ref=gate_in.at[member],
            send_sem=gate_send.at[away], recv_sem=gate_recv.at[away],
            device_id=(rank, target), device_id_type=MESH,
        )

    def part_copy(i, away, a):
        target = lax.rem(member + away, members)
        return pltpu.make_async_remote_copy(
            src_ref=sources[a].at[:, columns(target, i)], dst_ref=parts[a].at[i, member],
            send_sem=part_send.at[i, away, a], recv_sem=part_recv.at[i, away, a],
            device_id=(rank, target), device_id_type=MESH,
        )

    def part_arrival(i, away, a):
        origin = lax.rem(member + members - away, members)
        return pltpu.make_async_remote_copy(
            src_ref=sources[a].at[:, columns(origin, i)], dst_ref=parts[a].at[i, origin],
            send_sem=part_send.at[i, away, a], recv_sem=part_recv.at[i, away, a],
            device_id=(rank, origin), device_id_type=MESH,
        )

    def own_copy(i, a):
        return pltpu.make_async_copy(
            sources[a].at[:, columns(member, i)], parts[a].at[i, member], own_sem.at[i, a]
        )

    def state_copy(i):
        return pltpu.make_async_remote_copy(
            src_ref=state_out.at[i], dst_ref=state_in.at[i],
            send_sem=state_send.at[i], recv_sem=state_recv.at[i],
            device_id=(following, member), device_id_type=MESH,
        )

    def out_copy(i, away):
        target = lax.rem(member + away, members)
        return pltpu.make_async_remote_copy(
            src_ref=staged.at[i, target], dst_ref=out_ref.at[:, columns(member, i)],
            send_sem=out_send.at[i, away], recv_sem=out_recv.at[i, away],
            device_id=(rank, target), device_id_type=MESH,
        )

    def out_arrival(i, away):
        origin = lax.rem(member + members - away, members)
        return pltpu.make_async_remote_copy(
            src_ref=staged.at[i, origin], dst_ref=out_ref.at[:, columns(origin, i)],
            send_sem=out_send.at[i, away], recv_sem=out_recv.at[i, away],
            device_id=(rank, origin), device_id_type=MESH,
        )

    def own_out_copy(i):
        return pltpu.make_async_copy(
            staged.at[i, member], out_ref.at[:, columns(member, i)], own_out.at[i]
        )

    own_gate = pltpu.make_async_copy(gate_ref.at[member], gate_in.at[member], gate_recv.at[0])
    own_gate.start()
    for away in range(1, members):
        gate_copy(away).start()

    @pl.loop(0, heads)
    def _(i):
        for a in (1, 0, 2):
            for away in range(1, members):
                part_copy(i, away, a).start()
            own_copy(i, a).start()

    row = lax.broadcasted_iota(jnp.int32, (LANES, LANES), 0)
    col = lax.broadcasted_iota(jnp.int32, (LANES, LANES), 1)
    own_gate.wait()
    for away in range(1, members):
        gate_copy(away).wait()
    until = jnp.where(row >= col, 1.0, 0.0).astype(BF16)
    until_t = jnp.where(row <= col, 1.0, 0.0).astype(BF16)
    for b in range(members):
        cum[b] = dot(until, gate_in[b, 0])
        cum_t[b] = dot(gate_in[b, 1], until_t)
        beta_t[b] = gate_in[b, 1].astype(F32)

    @pl.loop(0, heads)
    def _(i):
        for a in range(3):
            for away in range(1, members):
                part_arrival(i, away, a).wait_recv()
            own_copy(i, a).wait()
        maps = []
        for b in range(members):
            beta_col = jnp.sum(
                jnp.where(col == i, gate_in[b, 0].astype(F32), 0.0), axis=1, keepdims=True
            )
            cum_col = jnp.sum(jnp.where(col == heads + i, cum[b], 0.0), axis=1, keepdims=True)
            maps.append(
                block_maps(
                    k_in[i, b], q_in[i, b], v_in[i, b],
                    beta_col, beta_t[b, pl.ds(i, 1), :],
                    cum_col, cum_t[b, pl.ds(heads + i, 1), :], row, col,
                )
            )
        query, output, move, left = maps[0]
        read_map[0], read_base[0] = query, output
        moved = jnp.concatenate([move, left], axis=1)
        for b in range(1, members):
            query, output, move, left = maps[b]
            both = dot3(jnp.concatenate([move, query], axis=0), moved)
            read_map[b] = both[LANES:, :LANES]
            read_base[b] = both[LANES:, LANES:] + output
            moved = jnp.concatenate([both[:LANES, :LANES], both[:LANES, LANES:] + left], axis=1)
        total_map, total_base = left3(moved[:, :LANES]), moved[:, LANES:]

        @pl.when(rank > 0)
        def _():
            state_copy(i).wait_recv()

        @pl.when(rank == 0)
        def _():
            state_in[i] = jnp.zeros((LANES, LANES), F32)

        entering = right3(state_in[i])
        state_out[i] = total_base + dot(total_map, entering)

        @pl.when(rank < ranks - 1)
        def _():
            state_copy(i).start()

        for b in range(members):
            staged[i, b] = (read_base[b] + dot(left3(read_map[b]), entering)).astype(BF16)
        for away in range(1, members):
            out_copy(i, away).start()
        own_out_copy(i).start()

    @pl.loop(0, heads)
    def _(i):
        for away in range(1, members):
            for a in range(3):
                part_copy(i, away, a).wait_send()
            out_copy(i, away).wait_send()
            out_arrival(i, away).wait_recv()
        own_out_copy(i).wait()

        @pl.when(rank < ranks - 1)
        def _():
            state_copy(i).wait_send()


def shards(ranks, members, query_rows, key_rows, value_rows, write_rate, log_decay):
    tokens, all_heads = write_rate.shape
    heads = all_heads // members
    both = jnp.stack(
        [write_rate.reshape(tokens, members, heads), log_decay.reshape(tokens, members, heads)], axis=2
    ).reshape(tokens, members, 2 * heads)
    both = jnp.pad(jnp.swapaxes(both, 0, 1), ((0, 0), (0, 0), (0, LANES - 2 * heads)))
    gates = jnp.stack([both, jnp.swapaxes(both, 1, 2)], axis=1)
    anywhere = pl.BlockSpec(memory_space=pl.ANY)
    part = pltpu.VMEM((heads, members, tokens, LANES), BF16)
    square = pltpu.VMEM((members, LANES, LANES), F32)
    state = pltpu.VMEM((heads, LANES, LANES), F32)
    dma = pltpu.SemaphoreType.DMA
    return pl.pallas_call(
        functools.partial(kernel, ranks, members, heads),
        out_shape=jax.ShapeDtypeStruct(value_rows.shape, BF16),
        in_specs=[anywhere] * 4,
        out_specs=anywhere,
        scratch_shapes=[
            part, part, part,
            pltpu.VMEM((members, 2, LANES, LANES), BF16),
            square, square, square,
            state, state,
            square, square,
            part,
            dma((members,)), dma((members,)),
            dma((heads, members, 3)), dma((heads, members, 3)), dma((heads, 3)),
            dma((heads,)), dma((heads,)),
            dma((heads, members)), dma((heads, members)), dma((heads,)),
        ],
        compiler_params=pltpu.CompilerParams(
            collective_id=0, has_side_effects=True, vmem_limit_bytes=40 * 1024 * 1024
        ),
        cost_estimate=pl.CostEstimate(flops=10**10, bytes_accessed=2**23, transcendentals=0),
    )(query_rows, key_rows, value_rows, gates)


def solution(mesh):
    placed = P(("seq", "head"), None)
    return jax.shard_map(
        functools.partial(shards, mesh.shape["seq"], mesh.shape["head"]),
        mesh=mesh, in_specs=(placed,) * 5, out_specs=placed, check_vma=False,
    )
```

```python
import functools

import jax
import jax.numpy as jnp
from jax import lax
from jax.experimental import pallas as pl
from jax.experimental.pallas import tpu as pltpu
from jax.sharding import PartitionSpec as P

LANES = 128
EPSILON = 1e-06
MESH = pl.DeviceIdType.MESH
F32 = jnp.float32
BF16 = jnp.bfloat16


def halves(x):
    high = x.astype(BF16)
    return high, (x - high.astype(F32)).astype(BF16)


def dot(a, b):
    return jnp.dot(a, b, preferred_element_type=F32)


def dot_t(a, b, dims):
    return lax.dot_general(a, b, (dims, ((), ())), preferred_element_type=F32)


def left3(a):
    high, low = halves(a)
    return jnp.concatenate([high, low, high], axis=1)


def right3(b):
    high, low = halves(b)
    return jnp.concatenate([high, high, low], axis=0)


def dot3(a, b):
    return dot(left3(a), right3(b))


def blockwise(compact, row, col, size):
    whole = jnp.concatenate([compact] * (LANES // size), axis=0)
    return jnp.where((row ^ col) < size, whole, 0.0)


def side_by_side(matrix, size):
    return functools.reduce(jnp.add, [matrix[at : at + size] for at in range(0, LANES, size)])


def unit_lower_inverses(lowers, row, col):
    apart = row ^ col
    small = 32

    def corner(lower, span):
        return jnp.where((apart >= span) & (apart < 2 * span), lower, 0.0)

    unit = jnp.where(row == col, 1.0, 0.0)
    found = [unit - corner(lower, 1) for lower in lowers]
    packed = [side_by_side(x, small) for x in found]
    span = 2
    while span < small:
        corners = [side_by_side(corner(lower, span), small) for lower in lowers]
        whole = [right3(blockwise(x, row, col, small)) for x in packed]
        partial = [dot(left3(c), w) for c, w in zip(corners, whole)]
        whole = [right3(blockwise(x, row, col, small)) for x in partial]
        packed = [x - dot(left3(x), w) for x, w in zip(packed, whole)]
        span *= 2
    found = [blockwise(x, row, col, small) for x in packed]
    while span < LANES:
        odd = range(span, LANES, 2 * span)
        lefts = [
            left3(jnp.concatenate([corner(lower, span)[at : at + span] for at in odd], axis=0))
            for lower in lowers
        ]
        partial = [dot(c, right3(x)) for c, x in zip(lefts, found)]
        nothing = jnp.zeros((span, LANES), F32)
        spread = [
            right3(
                jnp.concatenate(
                    [
                        piece
                        for n in range(len(odd))
                        for piece in (nothing, x[n * span : (n + 1) * span])
                    ],
                    axis=0,
                )
            )
            for x in partial
        ]
        lefts = [left3(jnp.concatenate([x[at : at + span] for at in odd], axis=0)) for x in found]
        change = [dot(x, w) for x, w in zip(lefts, spread)]
        found = [
            jnp.concatenate(
                [
                    piece
                    for n, at in enumerate(odd)
                    for piece in (
                        x[at - span : at], x[at : at + span] - c[n * span : (n + 1) * span]
                    )
                ],
                axis=0,
            )
            for x, c in zip(found, change)
        ]
        span *= 2
    return found


def block_maps(units, row, col):
    prepared = []
    for keys, queries, values, beta_col, beta_row, cum_col, cum_row in units:
        keys_t = keys.T
        products = dot(jnp.concatenate([keys, queries], axis=0), keys_t)
        gram, raw_scores = products[:LANES], products[LANES:]
        diagonal = jnp.where(row == col, gram, 0.0)
        r_col = lax.rsqrt(jnp.sum(diagonal, axis=1, keepdims=True) + EPSILON)
        r_row = lax.rsqrt(jnp.sum(diagonal, axis=0, keepdims=True) + EPSILON)
        within = row >= col
        ratios = jnp.where(within, jnp.exp(jnp.where(within, cum_col - cum_row, 0.0)), 0.0)
        faded = ratios * r_row
        lower = jnp.where(row > col, gram * faded * (beta_col * r_col), 0.0)
        prepared.append((keys_t, lower, raw_scores * faded, r_col, r_row))
    inverses = unit_lower_inverses([p[1] for p in prepared], row, col)
    maps = []
    for unit, (keys_t, _, scores, r_col, r_row), inverse in zip(units, prepared, inverses):
        keys, queries, values, _, beta_row, cum_col, cum_row = unit
        end_log = cum_row[:, LANES - 1 :]
        for_values = jnp.concatenate(halves(inverse * beta_row), axis=1)
        for_keys = jnp.concatenate(halves(inverse * (beta_row * jnp.exp(cum_row) * r_row)), axis=1)
        base = dot(for_values, jnp.concatenate([values, values], axis=0))
        wy = dot(for_keys, jnp.concatenate([keys, keys], axis=0))
        solved = jnp.concatenate([wy, base], axis=1)
        read = dot3(scores, solved)
        carried = solved * (r_col * jnp.exp(end_log - cum_col))
        left = dot(
            jnp.concatenate([keys_t, keys_t], axis=1), jnp.concatenate(halves(carried), axis=0)
        )
        move = jnp.where(row == col, jnp.exp(end_log), 0.0) - left[:, :LANES]
        query = queries.astype(F32) * jnp.exp(cum_col) - read[:, :LANES]
        maps.append((query, read[:, LANES:], move, left[:, LANES:]))
    return maps


def kernel(
    ranks, members, heads,
    q_ref, k_ref, v_ref, gate_ref,
    out_ref,
    q_in, k_in, v_in, gate_in, cum, cum_t, beta_t, state_in, state_out, read_map, read_base, staged,
    gate_send, gate_recv, part_send, part_recv, own_sem,
    state_send, state_recv, out_send, out_recv, own_out,
):
    rank, member = lax.axis_index("seq"), lax.axis_index("head")
    following, leading = lax.rem(rank + 1, ranks), lax.rem(rank + ranks - 1, ranks)
    sources, parts = (q_ref, k_ref, v_ref), (q_in, k_in, v_in)

    barrier = pltpu.get_barrier_semaphore()
    for away in range(1, members):
        pl.semaphore_signal(
            barrier, inc=1, device_id=(rank, lax.rem(member + away, members)), device_id_type=MESH
        )
    for other in (following, leading):
        pl.semaphore_signal(barrier, inc=1, device_id=(other, member), device_id_type=MESH)
    pl.semaphore_wait(barrier, members + 1)

    def columns(owner, i):
        return pl.ds(pl.multiple_of((owner * heads + i) * LANES, LANES), LANES)

    def gate_copy(away):
        target = lax.rem(member + away, members)
        return pltpu.make_async_remote_copy(
            src_ref=gate_ref.at[target], dst_ref=gate_in.at[member],
            send_sem=gate_send.at[away], recv_sem=gate_recv.at[away],
            device_id=(rank, target), device_id_type=MESH,
        )

    def part_copy(i, away, a):
        target = lax.rem(member + away, members)
        return pltpu.make_async_remote_copy(
            src_ref=sources[a].at[:, columns(target, i)], dst_ref=parts[a].at[i, member],
            send_sem=part_send.at[i, away, a], recv_sem=part_recv.at[i, away, a],
            device_id=(rank, target), device_id_type=MESH,
        )

    def part_arrival(i, away, a):
        origin = lax.rem(member + members - away, members)
        return pltpu.make_async_remote_copy(
            src_ref=sources[a].at[:, columns(origin, i)], dst_ref=parts[a].at[i, origin],
            send_sem=part_send.at[i, away, a], recv_sem=part_recv.at[i, away, a],
            device_id=(rank, origin), device_id_type=MESH,
        )

    def own_copy(i, a):
        return pltpu.make_async_copy(
            sources[a].at[:, columns(member, i)], parts[a].at[i, member], own_sem.at[i, a]
        )

    def state_copy(i):
        return pltpu.make_async_remote_copy(
            src_ref=state_out.at[i], dst_ref=state_in.at[i],
            send_sem=state_send.at[i], recv_sem=state_recv.at[i],
            device_id=(following, member), device_id_type=MESH,
        )

    def out_copy(i, away):
        target = lax.rem(member + away, members)
        return pltpu.make_async_remote_copy(
            src_ref=staged.at[i, target], dst_ref=out_ref.at[:, columns(member, i)],
            send_sem=out_send.at[i, away], recv_sem=out_recv.at[i, away],
            device_id=(rank, target), device_id_type=MESH,
        )

    def out_arrival(i, away):
        origin = lax.rem(member + members - away, members)
        return pltpu.make_async_remote_copy(
            src_ref=staged.at[i, origin], dst_ref=out_ref.at[:, columns(origin, i)],
            send_sem=out_send.at[i, away], recv_sem=out_recv.at[i, away],
            device_id=(rank, origin), device_id_type=MESH,
        )

    def own_out_copy(i):
        return pltpu.make_async_copy(
            staged.at[i, member], out_ref.at[:, columns(member, i)], own_out.at[i]
        )

    own_gate = pltpu.make_async_copy(gate_ref.at[member], gate_in.at[member], gate_recv.at[0])
    own_gate.start()
    for away in range(1, members):
        gate_copy(away).start()

    @pl.loop(0, heads)
    def _(i):
        for a in (1, 0, 2):
            for away in range(1, members):
                part_copy(i, away, a).start()
            own_copy(i, a).start()

    row = lax.broadcasted_iota(jnp.int32, (LANES, LANES), 0)
    col = lax.broadcasted_iota(jnp.int32, (LANES, LANES), 1)
    own_gate.wait()
    for away in range(1, members):
        gate_copy(away).wait()
    until = jnp.where(row >= col, 1.0, 0.0).astype(BF16)
    until_t = jnp.where(row <= col, 1.0, 0.0).astype(BF16)
    for b in range(members):
        cum[b] = dot(until, gate_in[b, 0])
        cum_t[b] = dot(gate_in[b, 1], until_t)
        beta_t[b] = gate_in[b, 1].astype(F32)

    @pl.loop(0, heads)
    def _(i):
        for a in range(3):
            for away in range(1, members):
                part_arrival(i, away, a).wait_recv()
            own_copy(i, a).wait()
        units = []
        for b in range(members):
            beta_col = jnp.sum(
                jnp.where(col == i, gate_in[b, 0].astype(F32), 0.0), axis=1, keepdims=True
            )
            cum_col = jnp.sum(jnp.where(col == heads + i, cum[b], 0.0), axis=1, keepdims=True)
            units.append(
                (
                    k_in[i, b], q_in[i, b], v_in[i, b],
                    beta_col, beta_t[b, pl.ds(i, 1), :],
                    cum_col, cum_t[b, pl.ds(heads + i, 1), :],
                )
            )
        maps = block_maps(units, row, col)
        query, output, move, left = maps[0]
        read_map[0], read_base[0] = query, output
        moved = jnp.concatenate([move, left], axis=1)
        for b in range(1, members):
            query, output, move, left = maps[b]
            both = dot3(jnp.concatenate([move, query], axis=0), moved)
            read_map[b] = both[LANES:, :LANES]
            read_base[b] = both[LANES:, LANES:] + output
            moved = jnp.concatenate([both[:LANES, :LANES], both[:LANES, LANES:] + left], axis=1)
        total_map, total_base = left3(moved[:, :LANES]), moved[:, LANES:]

        @pl.when(rank > 0)
        def _():
            state_copy(i).wait_recv()

        @pl.when(rank == 0)
        def _():
            state_in[i] = jnp.zeros((LANES, LANES), F32)

        entering = right3(state_in[i])
        state_out[i] = total_base + dot(total_map, entering)

        @pl.when(rank < ranks - 1)
        def _():
            state_copy(i).start()

        reading = left3(read_map[...].reshape(members * LANES, LANES))
        reached = read_base[...] + dot(reading, entering).reshape(members, LANES, LANES)
        staged[i] = reached.astype(BF16)
        for away in range(1, members):
            out_copy(i, away).start()
        own_out_copy(i).start()

    @pl.loop(0, heads)
    def _(i):
        for away in range(1, members):
            for a in range(3):
                part_copy(i, away, a).wait_send()
            out_copy(i, away).wait_send()
            out_arrival(i, away).wait_recv()
        own_out_copy(i).wait()

        @pl.when(rank < ranks - 1)
        def _():
            state_copy(i).wait_send()


def shards(ranks, members, query_rows, key_rows, value_rows, write_rate, log_decay):
    tokens, all_heads = write_rate.shape
    heads = all_heads // members
    both = jnp.stack(
        [write_rate.reshape(tokens, members, heads), log_decay.reshape(tokens, members, heads)], axis=2
    ).reshape(tokens, members, 2 * heads)
    both = jnp.pad(jnp.swapaxes(both, 0, 1), ((0, 0), (0, 0), (0, LANES - 2 * heads)))
    gates = jnp.stack([both, jnp.swapaxes(both, 1, 2)], axis=1)
    anywhere = pl.BlockSpec(memory_space=pl.ANY)
    part = pltpu.VMEM((heads, members, tokens, LANES), BF16)
    square = pltpu.VMEM((members, LANES, LANES), F32)
    state = pltpu.VMEM((heads, LANES, LANES), F32)
    dma = pltpu.SemaphoreType.DMA
    return pl.pallas_call(
        functools.partial(kernel, ranks, members, heads),
        out_shape=jax.ShapeDtypeStruct(value_rows.shape, BF16),
        in_specs=[anywhere] * 4,
        out_specs=anywhere,
        scratch_shapes=[
            part, part, part,
            pltpu.VMEM((members, 2, LANES, LANES), BF16),
            square, square, square,
            state, state,
            square, square,
            part,
            dma((members,)), dma((members,)),
            dma((heads, members, 3)), dma((heads, members, 3)), dma((heads, 3)),
            dma((heads,)), dma((heads,)),
            dma((heads, members)), dma((heads, members)), dma((heads,)),
        ],
        compiler_params=pltpu.CompilerParams(
            collective_id=0, has_side_effects=True, vmem_limit_bytes=60 * 1024 * 1024
        ),
        cost_estimate=pl.CostEstimate(flops=10**10, bytes_accessed=2**23, transcendentals=0),
    )(query_rows, key_rows, value_rows, gates)


def solution(mesh):
    placed = P(("seq", "head"), None)
    return jax.shard_map(
        functools.partial(shards, mesh.shape["seq"], mesh.shape["head"]),
        mesh=mesh, in_specs=(placed,) * 5, out_specs=placed, check_vma=False,
    )
```

```python
import functools

import jax
import jax.numpy as jnp
from jax import lax
from jax.experimental import pallas as pl
from jax.experimental.pallas import tpu as pltpu
from jax.sharding import PartitionSpec as P

LANES = 128
EPSILON = 1e-06
MESH = pl.DeviceIdType.MESH
F32 = jnp.float32
BF16 = jnp.bfloat16


def halves(x):
    high = x.astype(BF16)
    return high, (x - high.astype(F32)).astype(BF16)


def dot(a, b):
    return jnp.dot(a, b, preferred_element_type=F32)


def dot_t(a, b, dims):
    return lax.dot_general(a, b, (dims, ((), ())), preferred_element_type=F32)


def left3(a):
    high, low = halves(a)
    return jnp.concatenate([high, low, high], axis=1)


def right3(b):
    high, low = halves(b)
    return jnp.concatenate([high, high, low], axis=0)


def dot3(a, b):
    return dot(left3(a), right3(b))


def blockwise(compact, row, col, size):
    whole = jnp.concatenate([compact] * (LANES // size), axis=0)
    return jnp.where((row ^ col) < size, whole, 0.0)


def side_by_side(matrix, size):
    return functools.reduce(jnp.add, [matrix[at : at + size] for at in range(0, LANES, size)])


def unit_lower_inverses(lowers, row, col):
    apart = row ^ col
    small = 32

    def corner(lower, span):
        return jnp.where((apart >= span) & (apart < 2 * span), lower, 0.0)

    unit = jnp.where(row == col, 1.0, 0.0)
    found = [unit - corner(lower, 1) for lower in lowers]
    packed = [side_by_side(x, small) for x in found]
    span = 2
    while span < small:
        corners = [side_by_side(corner(lower, span), small) for lower in lowers]
        whole = [right3(blockwise(x, row, col, small)) for x in packed]
        partial = [dot(left3(c), w) for c, w in zip(corners, whole)]
        whole = [right3(blockwise(x, row, col, small)) for x in partial]
        packed = [x - dot(left3(x), w) for x, w in zip(packed, whole)]
        span *= 2
    found = [blockwise(x, row, col, small) for x in packed]
    while span < LANES:
        odd = range(span, LANES, 2 * span)
        lefts = [
            left3(jnp.concatenate([corner(lower, span)[at : at + span] for at in odd], axis=0))
            for lower in lowers
        ]
        partial = [dot(c, right3(x)) for c, x in zip(lefts, found)]
        nothing = jnp.zeros((span, LANES), F32)
        spread = [
            right3(
                jnp.concatenate(
                    [
                        piece
                        for n in range(len(odd))
                        for piece in (nothing, x[n * span : (n + 1) * span])
                    ],
                    axis=0,
                )
            )
            for x in partial
        ]
        lefts = [left3(jnp.concatenate([x[at : at + span] for at in odd], axis=0)) for x in found]
        change = [dot(x, w) for x, w in zip(lefts, spread)]
        found = [
            jnp.concatenate(
                [
                    piece
                    for n, at in enumerate(odd)
                    for piece in (
                        x[at - span : at], x[at : at + span] - c[n * span : (n + 1) * span]
                    )
                ],
                axis=0,
            )
            for x, c in zip(found, change)
        ]
        span *= 2
    return found


def fading(cum_col, cum_row, r_row, row, col):
    within = row >= col
    return jnp.where(within, jnp.exp(jnp.where(within, cum_col - cum_row, 0.0)), 0.0) * r_row


def block_moves(units, row, col):
    prepared = []
    for keys, values, beta_col, beta_row, cum_col, cum_row in units:
        keys_t = keys.T
        gram = dot(keys, keys_t)
        diagonal = jnp.where(row == col, gram, 0.0)
        r_col = lax.rsqrt(jnp.sum(diagonal, axis=1, keepdims=True) + EPSILON)
        r_row = lax.rsqrt(jnp.sum(diagonal, axis=0, keepdims=True) + EPSILON)
        faded = fading(cum_col, cum_row, r_row, row, col)
        lower = jnp.where(row > col, gram * faded * (beta_col * r_col), 0.0)
        prepared.append((keys_t, lower, r_col, r_row))
    inverses = unit_lower_inverses([p[1] for p in prepared], row, col)
    moves = []
    for unit, (keys_t, _, r_col, r_row), inverse in zip(units, prepared, inverses):
        keys, values, _, beta_row, cum_col, cum_row = unit
        end_log = cum_row[:, LANES - 1 :]
        for_values = jnp.concatenate(halves(inverse * beta_row), axis=1)
        for_keys = jnp.concatenate(halves(inverse * (beta_row * jnp.exp(cum_row) * r_row)), axis=1)
        base = dot(for_values, jnp.concatenate([values, values], axis=0))
        wy = dot(for_keys, jnp.concatenate([keys, keys], axis=0))
        solved = jnp.concatenate([wy, base], axis=1)
        carried = solved * (r_col * jnp.exp(end_log - cum_col))
        left = dot(
            jnp.concatenate([keys_t, keys_t], axis=1), jnp.concatenate(halves(carried), axis=0)
        )
        move = jnp.where(row == col, jnp.exp(end_log), 0.0) - left[:, :LANES]
        moves.append((solved, r_row, move, left[:, LANES:]))
    return moves


def kernel(
    ranks, members, heads,
    q_ref, k_ref, v_ref, gate_ref,
    out_ref,
    q_in, k_in, v_in, gate_in, cum, cum_t, beta_t, state_in, state_out, solutions, norms, moved_in, staged,
    gate_send, gate_recv, part_send, part_recv, own_sem,
    state_send, state_recv, out_send, out_recv, own_out,
):
    rank, member = lax.axis_index("seq"), lax.axis_index("head")
    following, leading = lax.rem(rank + 1, ranks), lax.rem(rank + ranks - 1, ranks)
    sources, parts = (q_ref, k_ref, v_ref), (q_in, k_in, v_in)

    barrier = pltpu.get_barrier_semaphore()
    for away in range(1, members):
        pl.semaphore_signal(
            barrier, inc=1, device_id=(rank, lax.rem(member + away, members)), device_id_type=MESH
        )
    for other in (following, leading):
        pl.semaphore_signal(barrier, inc=1, device_id=(other, member), device_id_type=MESH)
    pl.semaphore_wait(barrier, members + 1)

    def columns(owner, i):
        return pl.ds(pl.multiple_of((owner * heads + i) * LANES, LANES), LANES)

    def gate_copy(away):
        target = lax.rem(member + away, members)
        return pltpu.make_async_remote_copy(
            src_ref=gate_ref.at[target], dst_ref=gate_in.at[member],
            send_sem=gate_send.at[away], recv_sem=gate_recv.at[away],
            device_id=(rank, target), device_id_type=MESH,
        )

    def part_copy(i, away, a):
        target = lax.rem(member + away, members)
        return pltpu.make_async_remote_copy(
            src_ref=sources[a].at[:, columns(target, i)], dst_ref=parts[a].at[i, member],
            send_sem=part_send.at[i, away, a], recv_sem=part_recv.at[i, away, a],
            device_id=(rank, target), device_id_type=MESH,
        )

    def part_arrival(i, away, a):
        origin = lax.rem(member + members - away, members)
        return pltpu.make_async_remote_copy(
            src_ref=sources[a].at[:, columns(origin, i)], dst_ref=parts[a].at[i, origin],
            send_sem=part_send.at[i, away, a], recv_sem=part_recv.at[i, away, a],
            device_id=(rank, origin), device_id_type=MESH,
        )

    def own_copy(i, a):
        return pltpu.make_async_copy(
            sources[a].at[:, columns(member, i)], parts[a].at[i, member], own_sem.at[i, a]
        )

    def state_copy(i):
        return pltpu.make_async_remote_copy(
            src_ref=state_out.at[i], dst_ref=state_in.at[i],
            send_sem=state_send.at[i], recv_sem=state_recv.at[i],
            device_id=(following, member), device_id_type=MESH,
        )

    def out_copy(i, away):
        target = lax.rem(member + away, members)
        return pltpu.make_async_remote_copy(
            src_ref=staged.at[i, target], dst_ref=out_ref.at[:, columns(member, i)],
            send_sem=out_send.at[i, away], recv_sem=out_recv.at[i, away],
            device_id=(rank, target), device_id_type=MESH,
        )

    def out_arrival(i, away):
        origin = lax.rem(member + members - away, members)
        return pltpu.make_async_remote_copy(
            src_ref=staged.at[i, origin], dst_ref=out_ref.at[:, columns(origin, i)],
            send_sem=out_send.at[i, away], recv_sem=out_recv.at[i, away],
            device_id=(rank, origin), device_id_type=MESH,
        )

    def own_out_copy(i):
        return pltpu.make_async_copy(
            staged.at[i, member], out_ref.at[:, columns(member, i)], own_out.at[i]
        )

    own_gate = pltpu.make_async_copy(gate_ref.at[member], gate_in.at[member], gate_recv.at[0])
    own_gate.start()
    for away in range(1, members):
        gate_copy(away).start()

    @pl.loop(0, heads)
    def _(i):
        for a in (1, 2):
            for away in range(1, members):
                part_copy(i, away, a).start()
            own_copy(i, a).start()

    @pl.loop(0, heads)
    def _(i):
        for away in range(1, members):
            part_copy(i, away, 0).start()
        own_copy(i, 0).start()

    row = lax.broadcasted_iota(jnp.int32, (LANES, LANES), 0)
    col = lax.broadcasted_iota(jnp.int32, (LANES, LANES), 1)
    own_gate.wait()
    for away in range(1, members):
        gate_copy(away).wait()
    until = jnp.where(row >= col, 1.0, 0.0).astype(BF16)
    until_t = jnp.where(row <= col, 1.0, 0.0).astype(BF16)
    for b in range(members):
        cum[b] = dot(until, gate_in[b, 0])
        cum_t[b] = dot(gate_in[b, 1], until_t)
        beta_t[b] = gate_in[b, 1].astype(F32)

    def decays(i, b):
        cum_col = jnp.sum(jnp.where(col == heads + i, cum[b], 0.0), axis=1, keepdims=True)
        return cum_col, cum_t[b, pl.ds(heads + i, 1), :]

    def arrived(i, arrays):
        for a in arrays:
            for away in range(1, members):
                part_arrival(i, away, a).wait_recv()
            own_copy(i, a).wait()

    def pass_on(i):
        @pl.when(rank > 0)
        def _():
            state_copy(i).wait_recv()

        @pl.when(rank == 0)
        def _():
            state_in[i] = jnp.zeros((LANES, LANES), F32)

        @pl.when(rank < ranks - 1)
        def _():
            total = moved_in[i, members - 1]
            state_out[i] = total[:, LANES:] + dot3(total[:, :LANES], state_in[i])
            state_copy(i).start()

    late = jnp.minimum(rank, heads)

    @pl.loop(0, heads)
    def _(i):
        arrived(i, (1, 2))
        units = []
        for b in range(members):
            beta_col = jnp.sum(
                jnp.where(col == i, gate_in[b, 0].astype(F32), 0.0), axis=1, keepdims=True
            )
            units.append(
                (k_in[i, b], v_in[i, b], beta_col, beta_t[b, pl.ds(i, 1), :], *decays(i, b))
            )
        moves = block_moves(units, row, col)
        moved = None
        for b, (solved, r_row, move, left) in enumerate(moves):
            solutions[i, b] = solved
            norms[i, b] = jnp.broadcast_to(r_row, (8, LANES))
            if moved is None:
                moved = jnp.concatenate([move, left], axis=1)
            else:
                both = dot3(move, moved)
                moved = jnp.concatenate([both[:, :LANES], both[:, LANES:] + left], axis=1)
            moved_in[i, b] = moved

        @pl.when(i >= late)
        def _():
            pass_on(i - late)

    @pl.loop(0, heads)
    def _(i):
        @pl.when(i < late)
        def _():
            pass_on(heads + i - late)

        arrived(i, (0,))
        entering = state_in[i]
        before = moved_in[i, : members - 1].reshape((members - 1) * LANES, 2 * LANES)
        later = dot(left3(before[:, :LANES]), right3(entering)) + before[:, LANES:]
        for b in range(members):
            cum_col, cum_row = decays(i, b)
            queries = q_in[i, b]
            faded = fading(cum_col, cum_row, norms[i, b, :1, :], row, col)
            scores = dot_t(queries, k_in[i, b], ((1,), (1,))) * faded
            read = dot3(scores, solutions[i, b])
            query = queries.astype(F32) * jnp.exp(cum_col) - read[:, :LANES]
            state = entering if b == 0 else later[(b - 1) * LANES : b * LANES]
            staged[i, b] = (read[:, LANES:] + dot3(query, state)).astype(BF16)
        for away in range(1, members):
            out_copy(i, away).start()
        own_out_copy(i).start()

    @pl.loop(0, heads)
    def _(i):
        for away in range(1, members):
            for a in range(3):
                part_copy(i, away, a).wait_send()
            out_copy(i, away).wait_send()
            out_arrival(i, away).wait_recv()
        own_out_copy(i).wait()

        @pl.when(rank < ranks - 1)
        def _():
            state_copy(i).wait_send()


def shards(ranks, members, query_rows, key_rows, value_rows, write_rate, log_decay):
    tokens, all_heads = write_rate.shape
    heads = all_heads // members
    both = jnp.stack(
        [write_rate.reshape(tokens, members, heads), log_decay.reshape(tokens, members, heads)], axis=2
    ).reshape(tokens, members, 2 * heads)
    both = jnp.pad(jnp.swapaxes(both, 0, 1), ((0, 0), (0, 0), (0, LANES - 2 * heads)))
    gates = jnp.stack([both, jnp.swapaxes(both, 1, 2)], axis=1)
    anywhere = pl.BlockSpec(memory_space=pl.ANY)
    part = pltpu.VMEM((heads, members, tokens, LANES), BF16)
    square = pltpu.VMEM((members, LANES, LANES), F32)
    state = pltpu.VMEM((heads, LANES, LANES), F32)
    dma = pltpu.SemaphoreType.DMA
    return pl.pallas_call(
        functools.partial(kernel, ranks, members, heads),
        out_shape=jax.ShapeDtypeStruct(value_rows.shape, BF16),
        in_specs=[anywhere] * 4,
        out_specs=anywhere,
        scratch_shapes=[
            part, part, part,
            pltpu.VMEM((members, 2, LANES, LANES), BF16),
            square, square, square,
            state, state,
            pltpu.VMEM((heads, members, LANES, 2 * LANES), F32),
            pltpu.VMEM((heads, members, 8, LANES), F32),
            pltpu.VMEM((heads, members, LANES, 2 * LANES), F32),
            part,
            dma((members,)), dma((members,)),
            dma((heads, members, 3)), dma((heads, members, 3)), dma((heads, 3)),
            dma((heads,)), dma((heads,)),
            dma((heads, members)), dma((heads, members)), dma((heads,)),
        ],
        compiler_params=pltpu.CompilerParams(
            collective_id=0, has_side_effects=True, vmem_limit_bytes=60 * 1024 * 1024
        ),
        cost_estimate=pl.CostEstimate(flops=10**10, bytes_accessed=2**23, transcendentals=0),
    )(query_rows, key_rows, value_rows, gates)


def solution(mesh):
    placed = P(("seq", "head"), None)
    return jax.shard_map(
        functools.partial(shards, mesh.shape["seq"], mesh.shape["head"]),
        mesh=mesh, in_specs=(placed,) * 5, out_specs=placed, check_vma=False,
    )
```

```python
import functools

import jax
import jax.numpy as jnp
from jax import lax
from jax.experimental import pallas as pl
from jax.experimental.pallas import tpu as pltpu
from jax.sharding import PartitionSpec as P

LANES = 128
EPSILON = 1e-06
MESH = pl.DeviceIdType.MESH
F32 = jnp.float32
BF16 = jnp.bfloat16


def halves(x):
    high = x.astype(BF16)
    return high, (x - high.astype(F32)).astype(BF16)


def dot(a, b):
    return jnp.dot(a, b, preferred_element_type=F32)


def dot_t(a, b, dims):
    return lax.dot_general(a, b, (dims, ((), ())), preferred_element_type=F32)


def left3(a):
    high, low = halves(a)
    return jnp.concatenate([high, low, high], axis=1)


def right3(b):
    high, low = halves(b)
    return jnp.concatenate([high, high, low], axis=0)


def dot3(a, b):
    return dot(left3(a), right3(b))


def blockwise(compact, row, col, size):
    whole = jnp.concatenate([compact] * (LANES // size), axis=0)
    return jnp.where((row ^ col) < size, whole, 0.0)


def side_by_side(matrix, size):
    return functools.reduce(jnp.add, [matrix[at : at + size] for at in range(0, LANES, size)])


def unit_lower_inverses(lowers, row, col):
    apart = row ^ col
    small = 32

    def corner(lower, span):
        return jnp.where((apart >= span) & (apart < 2 * span), lower, 0.0)

    unit = jnp.where(row == col, 1.0, 0.0)
    found = [unit - corner(lower, 1) for lower in lowers]
    packed = [side_by_side(x, small) for x in found]
    span = 2
    while span < small:
        corners = [side_by_side(corner(lower, span), small) for lower in lowers]
        whole = [right3(blockwise(x, row, col, small)) for x in packed]
        partial = [dot(left3(c), w) for c, w in zip(corners, whole)]
        whole = [right3(blockwise(x, row, col, small)) for x in partial]
        packed = [x - dot(left3(x), w) for x, w in zip(packed, whole)]
        span *= 2
    found = [blockwise(x, row, col, small) for x in packed]
    while span < LANES:
        odd = range(span, LANES, 2 * span)
        lefts = [
            left3(jnp.concatenate([corner(lower, span)[at : at + span] for at in odd], axis=0))
            for lower in lowers
        ]
        partial = [dot(c, right3(x)) for c, x in zip(lefts, found)]
        nothing = jnp.zeros((span, LANES), F32)
        spread = [
            right3(
                jnp.concatenate(
                    [
                        piece
                        for n in range(len(odd))
                        for piece in (nothing, x[n * span : (n + 1) * span])
                    ],
                    axis=0,
                )
            )
            for x in partial
        ]
        lefts = [left3(jnp.concatenate([x[at : at + span] for at in odd], axis=0)) for x in found]
        change = [dot(x, w) for x, w in zip(lefts, spread)]
        found = [
            jnp.concatenate(
                [
                    piece
                    for n, at in enumerate(odd)
                    for piece in (
                        x[at - span : at], x[at : at + span] - c[n * span : (n + 1) * span]
                    )
                ],
                axis=0,
            )
            for x, c in zip(found, change)
        ]
        span *= 2
    return found


def fading(cum_col, cum_row, r_row, row, col):
    within = row >= col
    return jnp.where(within, jnp.exp(jnp.where(within, cum_col - cum_row, 0.0)), 0.0) * r_row


def block_moves(units, row, col):
    prepared = []
    for keys, values, beta_col, beta_row, cum_col, cum_row in units:
        keys_t = keys.T
        gram = dot(keys, keys_t)
        diagonal = jnp.where(row == col, gram, 0.0)
        r_col = lax.rsqrt(jnp.sum(diagonal, axis=1, keepdims=True) + EPSILON)
        r_row = lax.rsqrt(jnp.sum(diagonal, axis=0, keepdims=True) + EPSILON)
        faded = fading(cum_col, cum_row, r_row, row, col)
        lower = jnp.where(row > col, gram * faded * (beta_col * r_col), 0.0)
        prepared.append((keys_t, lower, r_col, r_row))
    inverses = unit_lower_inverses([p[1] for p in prepared], row, col)
    moves = []
    for unit, (keys_t, _, r_col, r_row), inverse in zip(units, prepared, inverses):
        keys, values, _, beta_row, cum_col, cum_row = unit
        end_log = cum_row[:, LANES - 1 :]
        for_values = jnp.concatenate(halves(inverse * beta_row), axis=1)
        for_keys = jnp.concatenate(halves(inverse * (beta_row * jnp.exp(cum_row) * r_row)), axis=1)
        base = dot(for_values, jnp.concatenate([values, values], axis=0))
        wy = dot(for_keys, jnp.concatenate([keys, keys], axis=0))
        solved = jnp.concatenate([wy, base], axis=1)
        carried = solved * (r_col * jnp.exp(end_log - cum_col))
        left = dot(
            jnp.concatenate([keys_t, keys_t], axis=1), jnp.concatenate(halves(carried), axis=0)
        )
        move = jnp.where(row == col, jnp.exp(end_log), 0.0) - left[:, :LANES]
        moves.append((solved, r_row, move, left[:, LANES:]))
    return moves


def kernel(
    ranks, members, heads,
    q_ref, k_ref, v_ref, gate_ref,
    out_ref,
    q_in, k_in, v_in, gate_in, cum, cum_t, beta_t, state_in, state_out, solutions, norms, moved_in, staged,
    gate_send, gate_recv, part_send, part_recv, own_sem,
    state_send, state_recv, out_send, out_recv, own_out,
):
    rank, member = lax.axis_index("seq"), lax.axis_index("head")
    following, leading = lax.rem(rank + 1, ranks), lax.rem(rank + ranks - 1, ranks)
    sources, parts = (q_ref, k_ref, v_ref), (q_in, k_in, v_in)

    barrier = pltpu.get_barrier_semaphore()
    for away in range(1, members):
        pl.semaphore_signal(
            barrier, inc=1, device_id=(rank, lax.rem(member + away, members)), device_id_type=MESH
        )
    for other in (following, leading):
        pl.semaphore_signal(barrier, inc=1, device_id=(other, member), device_id_type=MESH)
    pl.semaphore_wait(barrier, members + 1)

    def columns(owner, i):
        return pl.ds(pl.multiple_of((owner * heads + i) * LANES, LANES), LANES)

    def gate_copy(away):
        target = lax.rem(member + away, members)
        return pltpu.make_async_remote_copy(
            src_ref=gate_ref.at[target], dst_ref=gate_in.at[member],
            send_sem=gate_send.at[away], recv_sem=gate_recv.at[away],
            device_id=(rank, target), device_id_type=MESH,
        )

    def part_copy(i, away, a):
        target = lax.rem(member + away, members)
        return pltpu.make_async_remote_copy(
            src_ref=sources[a].at[:, columns(target, i)], dst_ref=parts[a].at[i, member],
            send_sem=part_send.at[i, away, a], recv_sem=part_recv.at[i, away, a],
            device_id=(rank, target), device_id_type=MESH,
        )

    def part_arrival(i, away, a):
        origin = lax.rem(member + members - away, members)
        return pltpu.make_async_remote_copy(
            src_ref=sources[a].at[:, columns(origin, i)], dst_ref=parts[a].at[i, origin],
            send_sem=part_send.at[i, away, a], recv_sem=part_recv.at[i, away, a],
            device_id=(rank, origin), device_id_type=MESH,
        )

    def own_copy(i, a):
        return pltpu.make_async_copy(
            sources[a].at[:, columns(member, i)], parts[a].at[i, member], own_sem.at[i, a]
        )

    def state_copy(i):
        return pltpu.make_async_remote_copy(
            src_ref=state_out.at[i], dst_ref=state_in.at[i],
            send_sem=state_send.at[i], recv_sem=state_recv.at[i],
            device_id=(following, member), device_id_type=MESH,
        )

    def out_copy(i, away):
        target = lax.rem(member + away, members)
        return pltpu.make_async_remote_copy(
            src_ref=staged.at[i, target], dst_ref=out_ref.at[:, columns(member, i)],
            send_sem=out_send.at[i, away], recv_sem=out_recv.at[i, away],
            device_id=(rank, target), device_id_type=MESH,
        )

    def out_arrival(i, away):
        origin = lax.rem(member + members - away, members)
        return pltpu.make_async_remote_copy(
            src_ref=staged.at[i, origin], dst_ref=out_ref.at[:, columns(origin, i)],
            send_sem=out_send.at[i, away], recv_sem=out_recv.at[i, away],
            device_id=(rank, origin), device_id_type=MESH,
        )

    def own_out_copy(i):
        return pltpu.make_async_copy(
            staged.at[i, member], out_ref.at[:, columns(member, i)], own_out.at[i]
        )

    own_gate = pltpu.make_async_copy(gate_ref.at[member], gate_in.at[member], gate_recv.at[0])
    own_gate.start()
    for away in range(1, members):
        gate_copy(away).start()

    @pl.loop(0, heads)
    def _(i):
        for a in (1, 2):
            for away in range(1, members):
                part_copy(i, away, a).start()
            own_copy(i, a).start()

    @pl.loop(0, heads)
    def _(i):
        for away in range(1, members):
            part_copy(i, away, 0).start()
        own_copy(i, 0).start()

    row = lax.broadcasted_iota(jnp.int32, (LANES, LANES), 0)
    col = lax.broadcasted_iota(jnp.int32, (LANES, LANES), 1)
    own_gate.wait()
    for away in range(1, members):
        gate_copy(away).wait()
    until = jnp.where(row >= col, 1.0, 0.0).astype(BF16)
    until_t = jnp.where(row <= col, 1.0, 0.0).astype(BF16)
    for b in range(members):
        cum[b] = dot(until, gate_in[b, 0])
        cum_t[b] = dot(gate_in[b, 1], until_t)
        beta_t[b] = gate_in[b, 1].astype(F32)

    def decays(i, b):
        cum_col = jnp.sum(jnp.where(col == heads + i, cum[b], 0.0), axis=1, keepdims=True)
        return cum_col, cum_t[b, pl.ds(heads + i, 1), :]

    def arrived(i, arrays):
        for a in arrays:
            for away in range(1, members):
                part_arrival(i, away, a).wait_recv()
            own_copy(i, a).wait()

    def pass_on(i):
        total = moved_in[i, members - 1]
        total_map = left3(total[:, :LANES])

        @pl.when(rank > 0)
        def _():
            state_copy(i).wait_recv()

        @pl.when(rank == 0)
        def _():
            state_in[i] = jnp.zeros((LANES, LANES), F32)

        @pl.when(rank < ranks - 1)
        def _():
            state_out[i] = total[:, LANES:] + dot(total_map, right3(state_in[i]))
            state_copy(i).start()

    late = jnp.minimum(rank, heads)

    @pl.loop(0, heads)
    def _(i):
        arrived(i, (1, 2))
        units = []
        for b in range(members):
            beta_col = jnp.sum(
                jnp.where(col == i, gate_in[b, 0].astype(F32), 0.0), axis=1, keepdims=True
            )
            units.append(
                (k_in[i, b], v_in[i, b], beta_col, beta_t[b, pl.ds(i, 1), :], *decays(i, b))
            )
        moves = block_moves(units, row, col)
        moved = None
        for b, (solved, r_row, move, left) in enumerate(moves):
            solutions[i, b] = solved
            norms[i, b] = jnp.broadcast_to(r_row, (8, LANES))
            if moved is None:
                moved = jnp.concatenate([move, left], axis=1)
            else:
                both = dot3(move, moved)
                moved = jnp.concatenate([both[:, :LANES], both[:, LANES:] + left], axis=1)
            moved_in[i, b] = moved

        @pl.when(i >= late)
        def _():
            pass_on(i - late)

    @pl.loop(0, heads)
    def _(i):
        @pl.when(i < late)
        def _():
            pass_on(heads + i - late)

        arrived(i, (0,))
        entering = state_in[i]
        before = moved_in[i, : members - 1].reshape((members - 1) * LANES, 2 * LANES)
        later = dot(left3(before[:, :LANES]), right3(entering)) + before[:, LANES:]
        for b in range(members):
            cum_col, cum_row = decays(i, b)
            queries = q_in[i, b]
            faded = fading(cum_col, cum_row, norms[i, b, :1, :], row, col)
            scores = dot_t(queries, k_in[i, b], ((1,), (1,))) * faded
            read = dot3(scores, solutions[i, b])
            query = queries.astype(F32) * jnp.exp(cum_col) - read[:, :LANES]
            state = entering if b == 0 else later[(b - 1) * LANES : b * LANES]
            staged[i, b] = (read[:, LANES:] + dot3(query, state)).astype(BF16)
        for away in range(1, members):
            out_copy(i, away).start()
        own_out_copy(i).start()

    @pl.loop(0, heads)
    def _(i):
        for away in range(1, members):
            for a in range(3):
                part_copy(i, away, a).wait_send()
            out_copy(i, away).wait_send()
            out_arrival(i, away).wait_recv()
        own_out_copy(i).wait()

        @pl.when(rank < ranks - 1)
        def _():
            state_copy(i).wait_send()


def shards(ranks, members, query_rows, key_rows, value_rows, write_rate, log_decay):
    tokens, all_heads = write_rate.shape
    heads = all_heads // members
    both = jnp.stack(
        [write_rate.reshape(tokens, members, heads), log_decay.reshape(tokens, members, heads)], axis=2
    ).reshape(tokens, members, 2 * heads)
    both = jnp.pad(jnp.swapaxes(both, 0, 1), ((0, 0), (0, 0), (0, LANES - 2 * heads)))
    gates = jnp.stack([both, jnp.swapaxes(both, 1, 2)], axis=1)
    anywhere = pl.BlockSpec(memory_space=pl.ANY)
    part = pltpu.VMEM((heads, members, tokens, LANES), BF16)
    square = pltpu.VMEM((members, LANES, LANES), F32)
    state = pltpu.VMEM((heads, LANES, LANES), F32)
    dma = pltpu.SemaphoreType.DMA
    return pl.pallas_call(
        functools.partial(kernel, ranks, members, heads),
        out_shape=jax.ShapeDtypeStruct(value_rows.shape, BF16),
        in_specs=[anywhere] * 4,
        out_specs=pl.BlockSpec(memory_space=pltpu.VMEM),
        scratch_shapes=[
            part, part, part,
            pltpu.VMEM((members, 2, LANES, LANES), BF16),
            square, square, square,
            state, state,
            pltpu.VMEM((heads, members, LANES, 2 * LANES), F32),
            pltpu.VMEM((heads, members, 8, LANES), F32),
            pltpu.VMEM((heads, members, LANES, 2 * LANES), F32),
            part,
            dma((members,)), dma((members,)),
            dma((heads, members, 3)), dma((heads, members, 3)), dma((heads, 3)),
            dma((heads,)), dma((heads,)),
            dma((heads, members)), dma((heads, members)), dma((heads,)),
        ],
        compiler_params=pltpu.CompilerParams(
            collective_id=0, has_side_effects=True, vmem_limit_bytes=60 * 1024 * 1024
        ),
        cost_estimate=pl.CostEstimate(flops=10**10, bytes_accessed=2**23, transcendentals=0),
    )(query_rows, key_rows, value_rows, gates)


def solution(mesh):
    placed = P(("seq", "head"), None)
    return jax.shard_map(
        functools.partial(shards, mesh.shape["seq"], mesh.shape["head"]),
        mesh=mesh, in_specs=(placed,) * 5, out_specs=placed, check_vma=False,
    )
```
